32 devices in a mesh: groups: 2 (over x), events: 16 (over z, y, core).
Axes of the slice: x: 2, y: 2, z: 4, core: 2. Of those that a mesh axis runs over, the one named last changes fastest.
Arguments:
- waveforms: bfloat16 [64, 128, 1024], P(('groups', 'events')), parts along dimension 0, may hold values from -8 to 8
- matching: int32 [2, 32], P(None, 'groups'), parts along dimension 1, may hold values from 0 to 15, as said below
- available: int32 [64, 128, 2, 2], P(('groups', 'events')), parts along dimension 0, may hold values 0 or 1
Outputs:
- aligned_stack: bfloat16 [64, 128, 1024], P(('groups', 'events')), parts along dimension 0
- pair_scores: float32 [2, 64, 2, 128], P(None, ('groups', 'events')), parts along dimension 1
The draws below stay inside these ranges and needn't reach their ends.
There are 2 independent parts, one for each index of `groups`. The reference program is written for one: setup_inputs(seed, part) draws one part's arguments, and reference() takes and returns one part's arrays. A program takes and returns all parts, laid end to end along the dimension named above; each array names one. Nothing has to cross between parts.
Inputs may be any that keep to these rules, and one draw needn't show every extreme that they name: `matching`: in each round a block's partner is another block, and the partner of its partner is the block itself.
All inputs are finite; a program needn't handle non-finite values. No bound on the sum of `available` on one device may be relied on, other than what follows from the above.
Results may differ from the reference program's by a relative error of at most 0.018.
Values may be sent and summed in bfloat16 or wider, within the bound.
A program may use at most 128 MiB of HBM per device.

```python
import math
import jax
import jax.numpy as jnp
from jax import lax

EB = 2
STATIONS = 128
SAMPLES = 1024
LAGS = 128
ROUNDS = 2
MLEN = 1152
NBLK = 16
NEV = 32


def draw_waveforms(key, part):
    keys = jax.random.split(jax.random.fold_in(key, 7), 1)
    noise = jax.random.normal(keys[0], (NEV, STATIONS, SAMPLES), jnp.float32)
    wave = noise
    return jnp.clip(wave, -8.0, 8.0).astype(jnp.bfloat16)


def draw_matching(key, part):
    rounds_list = []
    for which in range(ROUNDS):
        order = jax.random.permutation(jax.random.fold_in(key, which + 11), NBLK).astype(jnp.int32)
        first = order[0::2]
        second = order[1::2]
        partner = jnp.zeros((NBLK,), jnp.int32).at[first].set(second).at[second].set(first)
        rounds_list.append(partner)
    return jnp.stack(rounds_list).astype(jnp.int32)


def set_ends(entries, stream_key, low, largest):
    longest = entries.shape.index(max(entries.shape))
    spots = []
    for shift in (0, 1):
        where = [jax.random.randint(jax.random.fold_in(stream_key, axis), (), 0, length) for axis, length in enumerate(entries.shape)]
        where[longest] = (where[longest] + shift) % entries.shape[longest]
        spots.append(tuple(where))
    return entries.at[spots[0]].set(low).at[spots[1]].set(largest)


def setup_inputs(seed: int = 0, part: int = 0) -> dict:
    arg_keys = jax.random.split(jax.random.key(seed), 4)
    part_keys = jax.random.split(jax.random.fold_in(arg_keys[3], part), 4)
    return {
        "waveforms": draw_waveforms(jax.random.fold_in(jax.random.fold_in(arg_keys[3], part), 71), part),
        "matching": draw_matching(jax.random.fold_in(jax.random.fold_in(arg_keys[3], part), 71), part),
        "available": set_ends((jax.random.randint(part_keys[2], (NEV, STATIONS, ROUNDS, EB), 0, 4) < 3).astype(jnp.int32), jax.random.fold_in(part_keys[2], 1), 0, 1),
    }


def make_tables():
    times = jnp.arange(SAMPLES, dtype=jnp.int32)
    freqs = jnp.arange(MLEN, dtype=jnp.int32)
    lagset = (jnp.arange(LAGS, dtype=jnp.int32) - LAGS // 2) % MLEN
    angle_t = (times[:, None] * freqs[None, :] % MLEN).astype(jnp.float32) * (2.0 * math.pi / MLEN)
    angle_l = (freqs[:, None] * lagset[None, :] % MLEN).astype(jnp.float32) * (2.0 * math.pi / MLEN)
    forward = jnp.concatenate([jnp.cos(angle_t), -jnp.sin(angle_t)], axis=1).astype(jnp.bfloat16)
    corr_tab = (jnp.concatenate([jnp.cos(angle_l), -jnp.sin(angle_l)], axis=0) / MLEN).astype(jnp.bfloat16)
    spread_tab = jnp.concatenate([jnp.cos(angle_l).T, jnp.sin(angle_l).T], axis=1).astype(jnp.bfloat16)
    back_tab = (jnp.concatenate([jnp.cos(angle_t).T, -jnp.sin(angle_t).T], axis=0) / MLEN).astype(jnp.bfloat16)
    return (forward, corr_tab, spread_tab, back_tab)

def cross_spectra(spec, partner):
    other = spec[partner].astype(jnp.float32)
    own = spec[None, :, None].astype(jnp.float32)
    real_a, imag_a = (own[..., :MLEN], own[..., MLEN:])
    real_b, imag_b = (other[..., :MLEN], other[..., MLEN:])
    return jnp.concatenate([real_a * real_b + imag_a * imag_b, real_a * imag_b - imag_a * real_b], axis=-1).astype(jnp.bfloat16)

def stack_of(spec, partner, spread, back_tab):
    other = spec[partner].astype(jnp.float32)
    real_y, imag_y = (other[..., :MLEN], other[..., MLEN:])
    real_v, imag_v = (spread[..., :MLEN], spread[..., MLEN:])
    real_z = lax.optimization_barrier(jnp.sum(real_v * real_y - imag_v * imag_y, axis=(0, 2)))
    imag_z = lax.optimization_barrier(jnp.sum(real_v * imag_y + imag_v * real_y, axis=(0, 2)))
    zspec = jnp.concatenate([real_z, imag_z], axis=-1).astype(jnp.bfloat16)
    flat = jnp.dot(zspec.reshape(-1, 2 * MLEN), back_tab, preferred_element_type=jnp.float32)
    return flat.reshape(zspec.shape[:-1] + (SAMPLES,)).astype(jnp.bfloat16)

def reference(waveforms, matching, available):
    forward, corr_tab, spread_tab, back_tab = make_tables()
    blocks_of = jnp.repeat(matching, EB, axis=1)
    partner = (blocks_of[:, :, None] * EB + jnp.arange(EB, dtype=jnp.int32)[None, None, :]).astype(jnp.int32)
    station_waves = jnp.moveaxis(waveforms, 1, 0)
    station_flags = jnp.moveaxis(available, 1, 0).astype(jnp.float32)

    def score_step(total, inputs):
        wave, flags = inputs
        spec = jnp.dot(wave, forward, preferred_element_type=jnp.float32).astype(jnp.bfloat16)
        cross = cross_spectra(spec, partner)
        corr = jnp.dot(cross.reshape(-1, 2 * MLEN), corr_tab, preferred_element_type=jnp.float32)
        corr = corr.reshape(ROUNDS, NEV, EB, LAGS)
        return (total + jnp.transpose(flags, (1, 0, 2))[..., None] * corr, spec)
    start = jnp.zeros((ROUNDS, NEV, EB, LAGS), jnp.float32)
    total, all_spec = lax.scan(score_step, start, (station_waves, station_flags))
    scores = total * (2.0 / math.sqrt(SAMPLES * STATIONS))
    weights = jax.nn.softmax(scores, axis=-1).astype(jnp.bfloat16)
    spread = jnp.dot(weights.reshape(-1, LAGS), spread_tab, preferred_element_type=jnp.float32)
    spread = spread.reshape(ROUNDS, NEV, EB, 2 * MLEN)

    def stack_step(carry, spec):
        return (carry, stack_of(spec, partner, spread, back_tab))
    stacks = lax.scan(stack_step, jnp.zeros((), jnp.float32), all_spec)[1]
    return (jnp.moveaxis(stacks, 0, 1), scores)
```

```python
import functools
import math

import jax
import jax.numpy as jnp
import ml_dtypes
import numpy as np
from jax import lax
from jax.experimental import pallas as pl
from jax.experimental.pallas import tpu as pltpu
from jax.sharding import PartitionSpec as P

LAGS = 128
LANES = 128
MESH = pl.DeviceIdType.MESH


def transform_length(samples):
    return samples + LAGS


def make_tables(samples):
    mlen = transform_length(samples)
    times = np.arange(samples, dtype=np.int64)
    freqs = np.arange(mlen, dtype=np.int64)
    lagset = (np.arange(LAGS, dtype=np.int64) - LAGS // 2) % mlen
    step = np.float32(2.0 * math.pi / mlen)
    angle_t = (times[:, None] * freqs[None, :] % mlen).astype(np.float32) * step
    angle_l = (freqs[:, None] * lagset[None, :] % mlen).astype(np.float32) * step
    return mlen, (np.cos(angle_t), np.sin(angle_t)), (np.cos(angle_l), np.sin(angle_l))


def full_tables(samples):
    mlen, (ct, st), (cl, sl) = make_tables(samples)
    bf = ml_dtypes.bfloat16
    return (
        np.concatenate([ct, -st], axis=1).astype(bf),
        (np.concatenate([cl, -sl], axis=0) / np.float32(mlen)).astype(bf),
        np.concatenate([cl.T, sl.T], axis=1).astype(bf),
        (np.concatenate([ct.T, -st.T], axis=0) / np.float32(mlen)).astype(bf),
    )


def half_tables(samples):
    mlen, (ct, st), (cl, sl) = make_tables(samples)
    bf = ml_dtypes.bfloat16
    bins = mlen // 2 + 1
    padded = -(-bins // LANES) * LANES
    twice = np.full((bins, 1), 2.0, np.float32)
    twice[0] = 1.0
    if mlen % 2 == 0:
        twice[-1] = 1.0

    def cols(x):
        return np.pad(x[:, :bins], ((0, 0), (0, padded - bins)))

    def rows(x):
        return np.pad(x[:bins] * twice / np.float32(mlen), ((0, padded - bins), (0, 0)))

    return padded, (
        np.concatenate([cols(ct), cols(-st)], axis=1).astype(bf),
        np.concatenate([rows(cl), rows(-sl)], axis=0).astype(bf),
        np.concatenate([cols(cl.T), cols(sl.T)], axis=1).astype(bf),
        np.concatenate([rows(ct.T), rows(-st.T)], axis=0).astype(bf),
    )


def kernel(
    n, eb, rounds, local, samples, bins, group, scale,
    match_ref, wave_ref, fwd_hbm, ctab_hbm, stab_hbm, back_hbm,
    out_ref, scores_ref,
    recv, fwd, ctab, stab, back, spec, cross, mask, part, score_in, wts, spread, zspec, sendb,
    tab_sem, own_sem, s1, r1, s2, r2, s3, r3, s4, r4,
):
    me = lax.axis_index("events")
    rows = eb * local
    pairs = rounds * eb * eb

    def ahead(k):
        return lax.rem(me + k, n)

    def behind(k):
        return lax.rem(me + n - k, n)

    tables = [
        pltpu.make_async_copy(src, dst, tab_sem.at[i])
        for i, (src, dst) in enumerate(
            ((fwd_hbm, fwd), (ctab_hbm, ctab), (stab_hbm, stab), (back_hbm, back))
        )
    ]
    own_in = pltpu.make_async_copy(wave_ref.at[me], recv.at[0], own_sem.at[0])
    own_in.start()
    for table in tables:
        table.start()

    barrier = pltpu.get_barrier_semaphore()

    @pl.loop(1, n)
    def _(k):
        pl.semaphore_signal(barrier, inc=1, device_id={"events": ahead(k)}, device_id_type=MESH)

    pl.semaphore_wait(barrier, n - 1)

    def wave_copy(k):
        return pltpu.make_async_remote_copy(
            src_ref=wave_ref.at[ahead(k)], dst_ref=recv.at[k], send_sem=s1.at[k],
            recv_sem=r1.at[k], device_id={"events": ahead(k)}, device_id_type=MESH,
        )

    def part_copy(k):
        return pltpu.make_async_remote_copy(
            src_ref=part.at[k], dst_ref=score_in.at[k], send_sem=s2.at[k],
            recv_sem=r2.at[k], device_id={"events": behind(k)}, device_id_type=MESH,
        )

    def weight_copy(k):
        return pltpu.make_async_remote_copy(
            src_ref=wts.at[0], dst_ref=wts.at[k], send_sem=s3.at[k],
            recv_sem=r3.at[k], device_id={"events": ahead(k)}, device_id_type=MESH,
        )

    def stack_copy(k):
        return pltpu.make_async_remote_copy(
            src_ref=sendb.at[k], dst_ref=out_ref.at[me], send_sem=s4.at[k],
            recv_sem=r4.at[k], device_id={"events": behind(k)}, device_id_type=MESH,
        )

    @pl.loop(1, n)
    def _(k):
        wave_copy(k).start()

    own_in.wait()
    tables[0].wait()

    def spectra(first):
        wave = recv[pl.ds(first, group), :, :samples].reshape(group * rows, samples)
        got = jnp.dot(wave, fwd[...], preferred_element_type=jnp.float32)
        spec[pl.ds(first * eb, group * eb)] = got.reshape(group * eb, local, 2 * bins)

    @pl.loop(0, n // group)
    def _(g):
        @pl.loop(0, group)
        def _(i):
            @pl.when(g * group + i > 0)
            def _():
                wave_copy(g * group + i).wait_recv()

        spectra(g * group)

    def partner_slot(r, c):
        return lax.rem(me + n - match_ref[r, behind(c)], n)

    @pl.loop(0, n)
    def _(c):
        flags = recv[c, :, samples:].astype(jnp.float32)
        for r in range(rounds):
            p = partner_slot(r, c)
            for e in range(eb):
                ar = spec[c * eb + e, :, :bins]
                ai = spec[c * eb + e, :, bins:]
                real, imag = [], []
                for j in range(eb):
                    br = spec[p * eb + j, :, :bins]
                    bi = spec[p * eb + j, :, bins:]
                    real.append(ar * br + ai * bi)
                    imag.append(ar * bi - ai * br)
                    lane = r * eb + j
                    flag = flags[e * local:(e + 1) * local, lane:lane + 1]
                    mask[c * pairs + (r * eb + e) * eb + j] = jnp.broadcast_to(flag, (local, LAGS))
                at = (c * rounds + r) * eb + e
                cross[at, :, :bins] = jnp.concatenate(real, axis=0).astype(jnp.bfloat16)
                cross[at, :, bins:] = jnp.concatenate(imag, axis=0).astype(jnp.bfloat16)

    tables[1].wait()

    @pl.loop(0, n // group)
    def _(g):
        block = cross[pl.ds(g * group * rounds * eb, group * rounds * eb)]
        corr = jnp.dot(
            block.reshape(group * pairs * local, 2 * bins), ctab[...],
            preferred_element_type=jnp.float32,
        ).reshape(group * pairs, local, LAGS)
        total = jnp.sum(corr * mask[pl.ds(g * group * pairs, group * pairs)], axis=1)
        part[pl.ds(g * group, group)] = total.reshape(group, pairs, LAGS)

    @pl.loop(1, n)
    def _(k):
        part_copy(k).start()

    @pl.loop(1, n)
    def _(k):
        part_copy(k).wait_recv()

    total = part[0]
    for k in range(1, n):
        total = total + score_in[k]
    scores = total * scale
    scores_ref[...] = scores
    grown = jnp.exp(scores - jnp.max(scores, axis=-1, keepdims=True))
    wts[0] = grown / jnp.sum(grown, axis=-1, keepdims=True)

    @pl.loop(1, n)
    def _(k):
        weight_copy(k).start()

    tables[2].wait()
    tables[3].wait()

    @pl.loop(1, n)
    def _(k):
        weight_copy(k).wait_recv()

    spread[...] = jnp.dot(
        wts[...].reshape(n * pairs, LAGS).astype(jnp.bfloat16), stab[...],
        preferred_element_type=jnp.float32,
    ).reshape(n, pairs, 2 * bins)

    @pl.loop(0, n // group)
    def _(g):
        @pl.loop(0, group)
        def _(i):
            c = g * group + i
            real = [None] * eb
            imag = [None] * eb
            for r in range(rounds):
                p = partner_slot(r, c)
                for j in range(eb):
                    yr = spec[p * eb + j, :, :bins]
                    yi = spec[p * eb + j, :, bins:]
                    for e in range(eb):
                        at = (r * eb + e) * eb + j
                        vr = spread[c, at:at + 1, :bins]
                        vi = spread[c, at:at + 1, bins:]
                        zr = vr * yr - vi * yi
                        zi = vr * yi + vi * yr
                        real[e] = zr if real[e] is None else real[e] + zr
                        imag[e] = zi if imag[e] is None else imag[e] + zi
            zspec[c, :, :bins] = jnp.concatenate(real, axis=0).astype(jnp.bfloat16)
            zspec[c, :, bins:] = jnp.concatenate(imag, axis=0).astype(jnp.bfloat16)

        got = jnp.dot(
            zspec[pl.ds(g * group, group)].reshape(group * rows, 2 * bins), back[...],
            preferred_element_type=jnp.float32,
        )
        sendb[pl.ds(g * group, group)] = got.astype(jnp.bfloat16).reshape(group, rows, samples)

        @pl.loop(0, group)
        def _(i):
            @pl.when(g * group + i > 0)
            def _():
                stack_copy(g * group + i).start()

    own_out = pltpu.make_async_copy(sendb.at[0], out_ref.at[me], own_sem.at[1])
    own_out.start()

    @pl.loop(1, n)
    def _(k):
        wave_copy(k).wait_send()
        part_copy(k).wait_send()
        weight_copy(k).wait_send()
        stack_copy(k).wait_send()
        stack_copy(k).wait_recv()

    own_out.wait()


def kernel_body(n, waveforms, matching, available):
    eb, stations, samples = waveforms.shape
    rounds = matching.shape[0]
    local = stations // n
    rows = eb * local
    pairs = rounds * eb * eb
    bins, tables = half_tables(samples)
    group = 4 if n % 4 == 0 else 1
    flags = available.astype(jnp.bfloat16).reshape(eb, stations, rounds * eb)
    flags = jnp.pad(flags, ((0, 0), (0, 0), (0, LANES - rounds * eb)))
    packed = jnp.concatenate([waveforms, flags], axis=-1)
    wide = samples + LANES
    packed = packed.reshape(eb, n, local, wide).transpose(1, 0, 2, 3).reshape(n, rows, wide)
    bf, f32 = jnp.bfloat16, jnp.float32
    vmem, dma = pltpu.VMEM, pltpu.SemaphoreType.DMA
    anywhere = pl.BlockSpec(memory_space=pl.ANY)
    stacks, scores = pl.pallas_call(
        functools.partial(
            kernel, n, eb, rounds, local, samples, bins, group,
            2.0 / math.sqrt(samples * stations),
        ),
        out_shape=(
            jax.ShapeDtypeStruct((n, rows, samples), bf),
            jax.ShapeDtypeStruct((pairs, LAGS), f32),
        ),
        in_specs=[pl.BlockSpec(memory_space=pltpu.SMEM)] + [anywhere] * 5,
        out_specs=(anywhere, pl.BlockSpec(memory_space=pltpu.VMEM)),
        scratch_shapes=[
            vmem((n, rows, wide), bf),
            vmem(tables[0].shape, bf),
            vmem(tables[1].shape, bf),
            vmem(tables[2].shape, bf),
            vmem(tables[3].shape, bf),
            vmem((n * eb, local, 2 * bins), f32),
            vmem((n * rounds * eb, rows, 2 * bins), bf),
            vmem((n * pairs, local, LAGS), f32),
            vmem((n, pairs, LAGS), f32),
            vmem((n, pairs, LAGS), f32),
            vmem((n, pairs, LAGS), f32),
            vmem((n, pairs, 2 * bins), f32),
            vmem((n, rows, 2 * bins), bf),
            vmem((n, rows, samples), bf),
            dma((4,)),
            dma((2,)),
        ] + [dma((n,))] * 8,
        compiler_params=pltpu.CompilerParams(
            collective_id=0, has_side_effects=True, vmem_limit_bytes=56 * 1024 * 1024
        ),
    )(matching, packed, *(jnp.asarray(t) for t in tables))
    stacks = stacks.reshape(n, eb, local, samples).transpose(1, 0, 2, 3)
    return stacks.reshape(eb, stations, samples), scores.reshape(rounds, eb, eb, LAGS)


def plain_body(waveforms, matching, available):
    eb, stations, samples = waveforms.shape
    mlen = transform_length(samples)
    forward, corr_tab, spread_tab, back_tab = (jnp.asarray(t) for t in full_tables(samples))
    rounds = matching.shape[0]
    flags = available.astype(jnp.bfloat16)
    held = lax.all_to_all(waveforms, "events", split_axis=1, concat_axis=0, tiled=True)
    held_flags = lax.all_to_all(flags, "events", split_axis=1, concat_axis=0, tiled=True)
    count, local = held.shape[:2]
    blocks = count // eb
    spectra = jnp.dot(
        held.reshape(count * local, samples), forward, preferred_element_type=jnp.float32
    )
    spectra = spectra.astype(jnp.bfloat16).reshape(count, local, 2 * mlen)
    chosen = (matching[:, :, None] == jnp.arange(blocks)[None, None, :]).astype(jnp.bfloat16)
    other = jnp.dot(
        chosen.reshape(rounds * blocks, blocks), spectra.reshape(blocks, eb * local * 2 * mlen),
        preferred_element_type=jnp.float32,
    ).reshape(rounds, blocks, 1, eb, local, 2 * mlen)
    own = spectra.reshape(1, blocks, eb, 1, local, 2 * mlen).astype(jnp.float32)
    real_a, imag_a = (own[..., :mlen], own[..., mlen:])
    real_b, imag_b = (other[..., :mlen], other[..., mlen:])
    cross = jnp.concatenate(
        [real_a * real_b + imag_a * imag_b, real_a * imag_b - imag_a * real_b], axis=-1
    ).astype(jnp.bfloat16)
    corr = jnp.dot(cross.reshape(-1, 2 * mlen), corr_tab, preferred_element_type=jnp.float32)
    corr = corr.reshape(rounds, count, eb, local, LAGS)
    weight_flags = jnp.transpose(held_flags, (2, 0, 3, 1)).astype(jnp.float32)
    totals = lax.psum(jnp.sum(weight_flags[..., None] * corr, axis=3), "events")
    all_scores = totals * (2.0 / math.sqrt(samples * stations))
    all_weights = jax.nn.softmax(all_scores, axis=-1).astype(jnp.bfloat16)
    scores = lax.dynamic_slice_in_dim(all_scores, lax.axis_index("events") * eb, eb, 1)
    spread = jnp.dot(all_weights.reshape(-1, LAGS), spread_tab, preferred_element_type=jnp.float32)
    spread = spread.reshape(rounds, blocks, eb, eb, 1, 2 * mlen)
    real_v, imag_v = (spread[..., :mlen], spread[..., mlen:])
    real_z = jnp.sum(real_v * real_b - imag_v * imag_b, axis=(0, 3))
    imag_z = jnp.sum(real_v * imag_b + imag_v * real_b, axis=(0, 3))
    zspec = jnp.concatenate([real_z, imag_z], axis=-1).astype(jnp.bfloat16)
    stacked = jnp.dot(zspec.reshape(-1, 2 * mlen), back_tab, preferred_element_type=jnp.float32)
    stacked = stacked.reshape(count, local, samples).astype(jnp.bfloat16)
    returned = lax.all_to_all(stacked, "events", split_axis=0, concat_axis=1, tiled=True)
    return (returned, scores)


def solution(mesh):
    n = mesh.shape["events"]
    placed = (
        P(("groups", "events"), None, None),
        P(None, "groups"),
        P(("groups", "events"), None, None, None),
    )

    def body(waveforms, matching, available):
        eb, stations, _ = waveforms.shape
        if stations % n == 0 and (stations // n) % 8 == 0 and eb * (stations // n) % 16 == 0:
            return kernel_body(n, waveforms, matching, available)
        return plain_body(waveforms, matching, available)

    return jax.shard_map(
        body,
        mesh=mesh,
        in_specs=placed,
        out_specs=(P(("groups", "events"), None, None), P(None, ("groups", "events"), None, None)),
        check_vma=False,
    )
```

```python
import functools
import math

import jax
import jax.numpy as jnp
import ml_dtypes
import numpy as np
from jax import lax
from jax.experimental import pallas as pl
from jax.experimental.pallas import tpu as pltpu
from jax.sharding import PartitionSpec as P

LAGS = 128
LANES = 128
MESH = pl.DeviceIdType.MESH


def transform_length(samples):
    return samples + LAGS


def make_tables(samples):
    mlen = transform_length(samples)
    times = np.arange(samples, dtype=np.int64)
    freqs = np.arange(mlen, dtype=np.int64)
    lagset = (np.arange(LAGS, dtype=np.int64) - LAGS // 2) % mlen
    step = np.float32(2.0 * math.pi / mlen)
    angle_t = (times[:, None] * freqs[None, :] % mlen).astype(np.float32) * step
    angle_l = (freqs[:, None] * lagset[None, :] % mlen).astype(np.float32) * step
    return mlen, (np.cos(angle_t), np.sin(angle_t)), (np.cos(angle_l), np.sin(angle_l))


def full_tables(samples):
    mlen, (ct, st), (cl, sl) = make_tables(samples)
    bf = ml_dtypes.bfloat16
    return (
        np.concatenate([ct, -st], axis=1).astype(bf),
        (np.concatenate([cl, -sl], axis=0) / np.float32(mlen)).astype(bf),
        np.concatenate([cl.T, sl.T], axis=1).astype(bf),
        (np.concatenate([ct.T, -st.T], axis=0) / np.float32(mlen)).astype(bf),
    )


def half_tables(samples):
    mlen, (ct, st), (cl, sl) = make_tables(samples)
    bf = ml_dtypes.bfloat16
    bins = mlen // 2 + 1
    padded = -(-bins // LANES) * LANES
    twice = np.full((bins, 1), 2.0, np.float32)
    twice[0] = 1.0
    if mlen % 2 == 0:
        twice[-1] = 1.0

    def cols(x):
        return np.pad(x[:, :bins], ((0, 0), (0, padded - bins)))

    def rows(x):
        return np.pad(x[:bins] * twice / np.float32(mlen), ((0, padded - bins), (0, 0)))

    return padded, (
        np.concatenate([cols(ct), cols(-st)], axis=1).astype(bf),
        np.concatenate([rows(cl), rows(-sl)], axis=0).astype(bf),
        np.concatenate([cols(cl.T), cols(sl.T)], axis=1).astype(bf),
        np.concatenate([rows(ct.T), rows(-st.T)], axis=0).astype(bf),
    )


def kernel(
    n, eb, rounds, local, stations, samples, bins, group, scale,
    match_ref, flag_ref, wave_hbm, fwd_hbm, ctab_hbm, stab_hbm, back_hbm,
    out_ref, scores_ref,
    wave, packed, recv, fwd, ctab, stab, back, spec, cross, part, score_in, wts, spread, zspec, sendb,
    tab_sem, own_sem, s1, r1, s2, r2, s3, r3, s4, r4,
):
    me = lax.axis_index("events")
    rows = eb * local
    pairs = rounds * eb * eb

    def ahead(k):
        return lax.rem(me + k, n)

    def behind(k):
        return lax.rem(me + n - k, n)

    tables = [
        pltpu.make_async_copy(src, dst, tab_sem.at[i])
        for i, (src, dst) in enumerate(
            ((fwd_hbm, fwd), (ctab_hbm, ctab), (stab_hbm, stab), (back_hbm, back))
        )
    ]
    own_in = pltpu.make_async_copy(wave_hbm, wave, own_sem.at[0])
    own_in.start()
    for table in tables:
        table.start()

    barrier = pltpu.get_barrier_semaphore()

    @pl.loop(1, n)
    def _(k):
        pl.semaphore_signal(barrier, inc=1, device_id={"events": ahead(k)}, device_id_type=MESH)

    flags = jnp.concatenate(
        [flag_ref[e, r] for r in range(rounds) for e in range(eb)], axis=0
    ).astype(jnp.float32)
    flags = jnp.concatenate(
        [flags, jnp.zeros((rows - pairs, stations), jnp.float32)], axis=0
    ).astype(jnp.bfloat16)
    own_in.wait()

    @pl.loop(0, n // 2)
    def _(q):
        traces = [
            wave[e, pl.ds(pl.multiple_of(q * 2 * local, 2 * local), 2 * local), :].astype(jnp.float32)
            for e in range(eb)
        ]
        for h in range(2):
            packed[2 * q + h, :, :samples] = jnp.concatenate(
                [t[h * local:(h + 1) * local] for t in traces], axis=0
            ).astype(jnp.bfloat16)
            packed[2 * q + h, :, samples:] = flags

    pl.semaphore_wait(barrier, n - 1)

    def wave_copy(k):
        return pltpu.make_async_remote_copy(
            src_ref=packed.at[ahead(k)], dst_ref=recv.at[k], send_sem=s1.at[k],
            recv_sem=r1.at[k], device_id={"events": ahead(k)}, device_id_type=MESH,
        )

    def part_copy(k):
        return pltpu.make_async_remote_copy(
            src_ref=part.at[k], dst_ref=score_in.at[k], send_sem=s2.at[k],
            recv_sem=r2.at[k], device_id={"events": behind(k)}, device_id_type=MESH,
        )

    def weight_copy(k):
        return pltpu.make_async_remote_copy(
            src_ref=wts.at[0], dst_ref=wts.at[k], send_sem=s3.at[k],
            recv_sem=r3.at[k], device_id={"events": ahead(k)}, device_id_type=MESH,
        )

    def stack_copy(k):
        return pltpu.make_async_remote_copy(
            src_ref=sendb.at[k], dst_ref=out_ref.at[me], send_sem=s4.at[k],
            recv_sem=r4.at[k], device_id={"events": behind(k)}, device_id_type=MESH,
        )

    @pl.loop(1, n)
    def _(k):
        wave_copy(k).start()

    recv[0] = packed[me]
    tables[0].wait()

    def spectra(first):
        wave = recv[pl.ds(first, group), :, :samples].reshape(group * rows, samples)
        got = jnp.dot(wave, fwd[...], preferred_element_type=jnp.float32)
        spec[pl.ds(first * eb, group * eb)] = got.reshape(group * eb, local, 2 * bins)

    @pl.loop(0, n // group)
    def _(g):
        @pl.loop(0, group)
        def _(i):
            @pl.when(g * group + i > 0)
            def _():
                wave_copy(g * group + i).wait_recv()

        spectra(g * group)

    def partner_slot(r, c):
        return lax.rem(me + n - match_ref[r, behind(c)], n)

    @pl.loop(0, n)
    def _(c):
        for r in range(rounds):
            p = partner_slot(r, c)
            for e in range(eb):
                ar = spec[c * eb + e, :, :bins]
                ai = spec[c * eb + e, :, bins:]
                real, imag = [], []
                for j in range(eb):
                    br = spec[p * eb + j, :, :bins]
                    bi = spec[p * eb + j, :, bins:]
                    real.append(ar * br + ai * bi)
                    imag.append(ar * bi - ai * br)
                at = (c * rounds + r) * eb + e
                cross[at, :, :bins] = jnp.concatenate(real, axis=0).astype(jnp.bfloat16)
                cross[at, :, bins:] = jnp.concatenate(imag, axis=0).astype(jnp.bfloat16)

    tables[1].wait()
    station = lax.broadcasted_iota(jnp.int32, (local, stations), 1)
    first = me * local + lax.broadcasted_iota(jnp.int32, (local, stations), 0)
    pick = jnp.where(station == first, 1.0, 0.0).astype(jnp.float32)
    ones = jnp.ones((stations, LAGS), jnp.bfloat16)

    @pl.loop(0, n // group)
    def _(g):
        block = cross[pl.ds(g * group * rounds * eb, group * rounds * eb)]
        corr = jnp.dot(
            block.reshape(group * pairs * local, 2 * bins), ctab[...],
            preferred_element_type=jnp.float32,
        ).reshape(group * pairs, local, LAGS)
        held = recv[pl.ds(g * group, group), :, samples:].astype(jnp.float32)[:, :pairs]
        held = held.reshape(group * pairs, 1, stations) * pick[None]
        mask = jnp.dot(
            held.reshape(group * pairs * local, stations).astype(jnp.bfloat16), ones,
            preferred_element_type=jnp.float32,
        ).reshape(group * pairs, local, LAGS)
        total = jnp.sum(corr * mask, axis=1)
        part[pl.ds(g * group, group)] = total.reshape(group, pairs, LAGS)

    @pl.loop(1, n)
    def _(k):
        part_copy(k).start()

    @pl.loop(1, n)
    def _(k):
        part_copy(k).wait_recv()

    total = part[0]
    for k in range(1, n):
        total = total + score_in[k]
    scores = total * scale
    for r in range(rounds):
        for e in range(eb):
            at = (r * eb + e) * eb
            scores_ref[r, e] = scores[at:at + eb]
    grown = jnp.exp(scores - jnp.max(scores, axis=-1, keepdims=True))
    wts[0] = grown / jnp.sum(grown, axis=-1, keepdims=True)

    @pl.loop(1, n)
    def _(k):
        weight_copy(k).start()

    tables[2].wait()
    tables[3].wait()

    @pl.loop(1, n)
    def _(k):
        weight_copy(k).wait_recv()

    spread[...] = jnp.dot(
        wts[...].reshape(n * pairs, LAGS).astype(jnp.bfloat16), stab[...],
        preferred_element_type=jnp.float32,
    ).reshape(n, pairs, 2 * bins)

    @pl.loop(0, n // group)
    def _(step):
        g = n // group - 1 - step

        @pl.loop(0, group)
        def _(i):
            c = g * group + i
            real = [None] * eb
            imag = [None] * eb
            for r in range(rounds):
                p = partner_slot(r, c)
                for j in range(eb):
                    yr = spec[p * eb + j, :, :bins]
                    yi = spec[p * eb + j, :, bins:]
                    for e in range(eb):
                        at = (r * eb + e) * eb + j
                        vr = spread[c, at:at + 1, :bins]
                        vi = spread[c, at:at + 1, bins:]
                        zr = vr * yr - vi * yi
                        zi = vr * yi + vi * yr
                        real[e] = zr if real[e] is None else real[e] + zr
                        imag[e] = zi if imag[e] is None else imag[e] + zi
            zspec[c, :, :bins] = jnp.concatenate(real, axis=0).astype(jnp.bfloat16)
            zspec[c, :, bins:] = jnp.concatenate(imag, axis=0).astype(jnp.bfloat16)

        got = jnp.dot(
            zspec[pl.ds(g * group, group)].reshape(group * rows, 2 * bins), back[...],
            preferred_element_type=jnp.float32,
        )
        sendb[pl.ds(g * group, group)] = got.astype(jnp.bfloat16).reshape(group, rows, samples)

        @pl.loop(0, group)
        def _(i):
            k = g * group + group - 1 - i

            @pl.when(k > 0)
            def _():
                stack_copy(k).start()

    own_out = pltpu.make_async_copy(sendb.at[0], out_ref.at[me], own_sem.at[1])
    own_out.start()

    @pl.loop(1, n)
    def _(k):
        wave_copy(k).wait_send()
        part_copy(k).wait_send()
        weight_copy(k).wait_send()
        stack_copy(k).wait_send()
        stack_copy(k).wait_recv()

    own_out.wait()


def kernel_body(n, waveforms, matching, available):
    eb, stations, samples = waveforms.shape
    rounds = matching.shape[0]
    local = stations // n
    rows = eb * local
    pairs = rounds * eb * eb
    bins, tables = half_tables(samples)
    group = 4 if n % 4 == 0 else 1
    wide = samples + stations
    bf, f32 = jnp.bfloat16, jnp.float32
    vmem, dma = pltpu.VMEM, pltpu.SemaphoreType.DMA
    anywhere = pl.BlockSpec(memory_space=pl.ANY)
    stacks, scores = pl.pallas_call(
        functools.partial(
            kernel, n, eb, rounds, local, stations, samples, bins, group,
            2.0 / math.sqrt(samples * stations),
        ),
        out_shape=(
            jax.ShapeDtypeStruct((n, rows, samples), bf),
            jax.ShapeDtypeStruct((rounds, eb, eb, LAGS), f32),
        ),
        in_specs=[
            pl.BlockSpec(memory_space=pltpu.SMEM),
            pl.BlockSpec(memory_space=pltpu.VMEM),
        ] + [anywhere] * 5,
        out_specs=(anywhere, pl.BlockSpec(memory_space=pltpu.VMEM)),
        scratch_shapes=[
            vmem((eb, stations, samples), bf),
            vmem((n, rows, wide), bf),
            vmem((n, rows, wide), bf),
            vmem(tables[0].shape, bf),
            vmem(tables[1].shape, bf),
            vmem(tables[2].shape, bf),
            vmem(tables[3].shape, bf),
            vmem((n * eb, local, 2 * bins), f32),
            vmem((n * rounds * eb, rows, 2 * bins), bf),
            vmem((n, pairs, LAGS), f32),
            vmem((n, pairs, LAGS), f32),
            vmem((n, pairs, LAGS), f32),
            vmem((n, pairs, 2 * bins), f32),
            vmem((n, rows, 2 * bins), bf),
            vmem((n, rows, samples), bf),
            dma((4,)),
            dma((2,)),
        ] + [dma((n,))] * 8,
        compiler_params=pltpu.CompilerParams(
            collective_id=0, has_side_effects=True, vmem_limit_bytes=56 * 1024 * 1024
        ),
    )(matching, available.transpose(0, 2, 3, 1), waveforms, *(jnp.asarray(t) for t in tables))
    stacks = stacks.reshape(n, eb, local, samples).transpose(1, 0, 2, 3)
    return stacks.reshape(eb, stations, samples), scores


def plain_body(waveforms, matching, available):
    eb, stations, samples = waveforms.shape
    mlen = transform_length(samples)
    forward, corr_tab, spread_tab, back_tab = (jnp.asarray(t) for t in full_tables(samples))
    rounds = matching.shape[0]
    flags = available.astype(jnp.bfloat16)
    held = lax.all_to_all(waveforms, "events", split_axis=1, concat_axis=0, tiled=True)
    held_flags = lax.all_to_all(flags, "events", split_axis=1, concat_axis=0, tiled=True)
    count, local = held.shape[:2]
    blocks = count // eb
    spectra = jnp.dot(
        held.reshape(count * local, samples), forward, preferred_element_type=jnp.float32
    )
    spectra = spectra.astype(jnp.bfloat16).reshape(count, local, 2 * mlen)
    chosen = (matching[:, :, None] == jnp.arange(blocks)[None, None, :]).astype(jnp.bfloat16)
    other = jnp.dot(
        chosen.reshape(rounds * blocks, blocks), spectra.reshape(blocks, eb * local * 2 * mlen),
        preferred_element_type=jnp.float32,
    ).reshape(rounds, blocks, 1, eb, local, 2 * mlen)
    own = spectra.reshape(1, blocks, eb, 1, local, 2 * mlen).astype(jnp.float32)
    real_a, imag_a = (own[..., :mlen], own[..., mlen:])
    real_b, imag_b = (other[..., :mlen], other[..., mlen:])
    cross = jnp.concatenate(
        [real_a * real_b + imag_a * imag_b, real_a * imag_b - imag_a * real_b], axis=-1
    ).astype(jnp.bfloat16)
    corr = jnp.dot(cross.reshape(-1, 2 * mlen), corr_tab, preferred_element_type=jnp.float32)
    corr = corr.reshape(rounds, count, eb, local, LAGS)
    weight_flags = jnp.transpose(held_flags, (2, 0, 3, 1)).astype(jnp.float32)
    totals = lax.psum(jnp.sum(weight_flags[..., None] * corr, axis=3), "events")
    all_scores = totals * (2.0 / math.sqrt(samples * stations))
    all_weights = jax.nn.softmax(all_scores, axis=-1).astype(jnp.bfloat16)
    scores = lax.dynamic_slice_in_dim(all_scores, lax.axis_index("events") * eb, eb, 1)
    spread = jnp.dot(all_weights.reshape(-1, LAGS), spread_tab, preferred_element_type=jnp.float32)
    spread = spread.reshape(rounds, blocks, eb, eb, 1, 2 * mlen)
    real_v, imag_v = (spread[..., :mlen], spread[..., mlen:])
    real_z = jnp.sum(real_v * real_b - imag_v * imag_b, axis=(0, 3))
    imag_z = jnp.sum(real_v * imag_b + imag_v * real_b, axis=(0, 3))
    zspec = jnp.concatenate([real_z, imag_z], axis=-1).astype(jnp.bfloat16)
    stacked = jnp.dot(zspec.reshape(-1, 2 * mlen), back_tab, preferred_element_type=jnp.float32)
    stacked = stacked.reshape(count, local, samples).astype(jnp.bfloat16)
    returned = lax.all_to_all(stacked, "events", split_axis=0, concat_axis=1, tiled=True)
    return (returned, scores)


def solution(mesh):
    n = mesh.shape["events"]
    placed = (
        P(("groups", "events"), None, None),
        P(None, "groups"),
        P(("groups", "events"), None, None, None),
    )

    def body(waveforms, matching, available):
        eb, stations, _ = waveforms.shape
        local = stations // n
        pairs = matching.shape[0] * eb * eb
        if n % 2 == 0 and stations % n == 0 and local % 8 == 0 and 8 <= pairs <= eb * local and (
            eb * local % 16 == 0 and stations % LANES == 0
        ):
            return kernel_body(n, waveforms, matching, available)
        return plain_body(waveforms, matching, available)

    return jax.shard_map(
        body,
        mesh=mesh,
        in_specs=placed,
        out_specs=(P(("groups", "events"), None, None), P(None, ("groups", "events"), None, None)),
        check_vma=False,
    )
```

```python
import functools
import math

import jax
import jax.numpy as jnp
import ml_dtypes
import numpy as np
from jax import lax
from jax.experimental import pallas as pl
from jax.experimental.pallas import tpu as pltpu
from jax.sharding import PartitionSpec as P

LAGS = 128
LANES = 128
MESH = pl.DeviceIdType.MESH


def transform_length(samples):
    return samples + LAGS


def make_tables(samples):
    mlen = transform_length(samples)
    times = np.arange(samples, dtype=np.int64)
    freqs = np.arange(mlen, dtype=np.int64)
    lagset = (np.arange(LAGS, dtype=np.int64) - LAGS // 2) % mlen
    step = np.float32(2.0 * math.pi / mlen)
    angle_t = (times[:, None] * freqs[None, :] % mlen).astype(np.float32) * step
    angle_l = (freqs[:, None] * lagset[None, :] % mlen).astype(np.float32) * step
    return mlen, (np.cos(angle_t), np.sin(angle_t)), (np.cos(angle_l), np.sin(angle_l))


def full_tables(samples):
    mlen, (ct, st), (cl, sl) = make_tables(samples)
    bf = ml_dtypes.bfloat16
    return (
        np.concatenate([ct, -st], axis=1).astype(bf),
        (np.concatenate([cl, -sl], axis=0) / np.float32(mlen)).astype(bf),
        np.concatenate([cl.T, sl.T], axis=1).astype(bf),
        (np.concatenate([ct.T, -st.T], axis=0) / np.float32(mlen)).astype(bf),
    )


def half_tables(samples):
    mlen, (ct, st), (cl, sl) = make_tables(samples)
    bf = ml_dtypes.bfloat16
    bins = mlen // 2 + 1
    padded = -(-bins // LANES) * LANES
    twice = np.full((bins, 1), 2.0, np.float32)
    twice[0] = 1.0
    if mlen % 2 == 0:
        twice[-1] = 1.0

    def cols(x):
        return np.pad(x[:, :bins], ((0, 0), (0, padded - bins)))

    def rows(x):
        return np.pad(x[:bins] * twice / np.float32(mlen), ((0, padded - bins), (0, 0)))

    return padded, (
        np.concatenate([cols(ct), cols(-st)], axis=1).astype(bf),
        np.concatenate([rows(cl), rows(-sl)], axis=0).astype(bf),
        np.concatenate([cols(cl.T), cols(sl.T)], axis=1).astype(bf),
        np.concatenate([rows(ct.T), rows(-st.T)], axis=0).astype(bf),
    )


def kernel(
    n, eb, rounds, local, stations, samples, bins, group, scale,
    match_ref, flag_ref, wave_hbm, fwd_hbm, ctab_hbm, stab_hbm, back_hbm,
    out_ref, scores_ref,
    wave, packed, recv, fwd, ctab, stab, back, spec, cross, part, score_in, wts, spread, zspec, sendb,
    tab_sem, own_sem, s1, r1, s2, r2, s3, r3, s4, r4,
):
    me = lax.axis_index("events")
    rows = eb * local
    pairs = rounds * eb * eb

    def ahead(k):
        return lax.rem(me + k, n)

    def behind(k):
        return lax.rem(me + n - k, n)

    tables = [
        pltpu.make_async_copy(src, dst, tab_sem.at[i])
        for i, (src, dst) in enumerate(
            ((fwd_hbm, fwd), (ctab_hbm, ctab), (stab_hbm, stab), (back_hbm, back))
        )
    ]
    own_in = pltpu.make_async_copy(wave_hbm, wave, own_sem.at[0])
    own_in.start()
    for table in tables:
        table.start()

    barrier = pltpu.get_barrier_semaphore()

    @pl.loop(1, n)
    def _(k):
        pl.semaphore_signal(barrier, inc=1, device_id={"events": ahead(k)}, device_id_type=MESH)

    flags = jnp.concatenate(
        [flag_ref[e, r] for r in range(rounds) for e in range(eb)], axis=0
    ).astype(jnp.float32)
    flags = jnp.concatenate(
        [flags, jnp.zeros((rows - pairs, stations), jnp.float32)], axis=0
    ).astype(jnp.bfloat16)
    own_in.wait()

    @pl.loop(0, n // 2)
    def _(q):
        traces = [
            wave[e, pl.ds(pl.multiple_of(q * 2 * local, 2 * local), 2 * local), :].astype(jnp.float32)
            for e in range(eb)
        ]
        for h in range(2):
            packed[2 * q + h, :, :samples] = jnp.concatenate(
                [t[h * local:(h + 1) * local] for t in traces], axis=0
            ).astype(jnp.bfloat16)
            packed[2 * q + h, :, samples:] = flags

    pl.semaphore_wait(barrier, n - 1)

    def wave_copy(k):
        return pltpu.make_async_remote_copy(
            src_ref=packed.at[ahead(k)], dst_ref=recv.at[k], send_sem=s1.at[k],
            recv_sem=r1.at[k], device_id={"events": ahead(k)}, device_id_type=MESH,
        )

    def part_copy(k):
        return pltpu.make_async_remote_copy(
            src_ref=part.at[k], dst_ref=score_in.at[k], send_sem=s2.at[k],
            recv_sem=r2.at[k], device_id={"events": behind(k)}, device_id_type=MESH,
        )

    def weight_copy(k):
        return pltpu.make_async_remote_copy(
            src_ref=wts.at[0], dst_ref=wts.at[k], send_sem=s3.at[k],
            recv_sem=r3.at[k], device_id={"events": ahead(k)}, device_id_type=MESH,
        )

    def stack_copy(k):
        return pltpu.make_async_remote_copy(
            src_ref=sendb.at[k], dst_ref=out_ref.at[me], send_sem=s4.at[k],
            recv_sem=r4.at[k], device_id={"events": behind(k)}, device_id_type=MESH,
        )

    @pl.loop(1, n)
    def _(k):
        wave_copy(k).start()

    recv[0] = packed[me]
    tables[0].wait()

    def spectra(first):
        wave = recv[pl.ds(first, group), :, :samples].reshape(group * rows, samples)
        got = jnp.dot(wave, fwd[...], preferred_element_type=jnp.float32)
        spec[pl.ds(first * eb, group * eb)] = got.reshape(group * eb, local, 2 * bins)

    @pl.loop(0, n // group)
    def _(g):
        @pl.loop(0, group)
        def _(i):
            @pl.when(g * group + i > 0)
            def _():
                wave_copy(g * group + i).wait_recv()

        spectra(g * group)

    def partner_slot(r, c):
        return lax.rem(me + n - match_ref[r, behind(c)], n)

    @pl.loop(0, n)
    def _(c):
        for r in range(rounds):
            p = partner_slot(r, c)
            for e in range(eb):
                ar = spec[c * eb + e, :, :bins]
                ai = spec[c * eb + e, :, bins:]
                real, imag = [], []
                for j in range(eb):
                    br = spec[p * eb + j, :, :bins]
                    bi = spec[p * eb + j, :, bins:]
                    real.append(ar * br + ai * bi)
                    imag.append(ar * bi - ai * br)
                at = (c * rounds + r) * eb + e
                cross[at, :, :bins] = jnp.concatenate(real, axis=0).astype(jnp.bfloat16)
                cross[at, :, bins:] = jnp.concatenate(imag, axis=0).astype(jnp.bfloat16)

    tables[1].wait()
    station = lax.broadcasted_iota(jnp.int32, (local, stations), 1)
    first = me * local + lax.broadcasted_iota(jnp.int32, (local, stations), 0)
    pick = jnp.where(station == first, 1.0, 0.0).astype(jnp.float32)
    ones = jnp.ones((stations, LAGS), jnp.bfloat16)

    @pl.loop(0, n // group)
    def _(g):
        block = cross[pl.ds(g * group * rounds * eb, group * rounds * eb)]
        corr = jnp.dot(
            block.reshape(group * pairs * local, 2 * bins), ctab[...],
            preferred_element_type=jnp.float32,
        ).reshape(group * pairs, local, LAGS)
        held = recv[pl.ds(g * group, group), :, samples:].astype(jnp.float32)[:, :pairs]
        held = held.reshape(group * pairs, 1, stations) * pick[None]
        mask = jnp.dot(
            held.reshape(group * pairs * local, stations).astype(jnp.bfloat16), ones,
            preferred_element_type=jnp.float32,
        ).reshape(group * pairs, local, LAGS)
        total = jnp.sum(corr * mask, axis=1)
        part[pl.ds(g * group, group)] = total.reshape(group, pairs, LAGS)

    @pl.loop(1, n)
    def _(k):
        part_copy(n - k).start()

    @pl.loop(1, n)
    def _(k):
        part_copy(n - k).wait_recv()

    total = part[0]
    for k in range(1, n):
        total = total + score_in[k]
    scores = total * scale
    for r in range(rounds):
        for e in range(eb):
            at = (r * eb + e) * eb
            scores_ref[r, e] = scores[at:at + eb]
    grown = jnp.exp(scores - jnp.max(scores, axis=-1, keepdims=True))
    wts[0] = grown / jnp.sum(grown, axis=-1, keepdims=True)

    @pl.loop(1, n)
    def _(k):
        weight_copy(k).start()

    tables[2].wait()
    tables[3].wait()

    @pl.loop(1, n)
    def _(k):
        weight_copy(k).wait_recv()

    spread[...] = jnp.dot(
        wts[...].reshape(n * pairs, LAGS).astype(jnp.bfloat16), stab[...],
        preferred_element_type=jnp.float32,
    ).reshape(n, pairs, 2 * bins)

    @pl.loop(0, n // group)
    def _(step):
        g = n // group - 1 - step

        @pl.loop(0, group)
        def _(i):
            c = g * group + i
            real = [None] * eb
            imag = [None] * eb
            for r in range(rounds):
                p = partner_slot(r, c)
                for j in range(eb):
                    yr = spec[p * eb + j, :, :bins]
                    yi = spec[p * eb + j, :, bins:]
                    for e in range(eb):
                        at = (r * eb + e) * eb + j
                        vr = spread[c, at:at + 1, :bins]
                        vi = spread[c, at:at + 1, bins:]
                        zr = vr * yr - vi * yi
                        zi = vr * yi + vi * yr
                        real[e] = zr if real[e] is None else real[e] + zr
                        imag[e] = zi if imag[e] is None else imag[e] + zi
            zspec[c, :, :bins] = jnp.concatenate(real, axis=0).astype(jnp.bfloat16)
            zspec[c, :, bins:] = jnp.concatenate(imag, axis=0).astype(jnp.bfloat16)

        got = jnp.dot(
            zspec[pl.ds(g * group, group)].reshape(group * rows, 2 * bins), back[...],
            preferred_element_type=jnp.float32,
        )
        sendb[pl.ds(g * group, group)] = got.astype(jnp.bfloat16).reshape(group, rows, samples)

        @pl.loop(0, group)
        def _(i):
            k = g * group + group - 1 - i

            @pl.when(k > 0)
            def _():
                stack_copy(k).start()

    own_out = pltpu.make_async_copy(sendb.at[0], out_ref.at[me], own_sem.at[1])
    own_out.start()

    @pl.loop(1, n)
    def _(k):
        wave_copy(k).wait_send()
        part_copy(k).wait_send()
        weight_copy(k).wait_send()
        stack_copy(k).wait_send()
        stack_copy(k).wait_recv()

    own_out.wait()


def finish(eb, local, stack_ref, score_ref, out_ref, scores_ref):
    scores_ref[...] = score_ref[...]

    @pl.loop(0, stack_ref.shape[0] // 2)
    def _(q):
        halves = [stack_ref[2 * q + h].astype(jnp.float32) for h in range(2)]
        for e in range(eb):
            out_ref[e, pl.ds(pl.multiple_of(q * 2 * local, 2 * local), 2 * local), :] = jnp.concatenate(
                [half[e * local:(e + 1) * local] for half in halves], axis=0
            ).astype(jnp.bfloat16)


def kernel_body(n, waveforms, matching, available):
    eb, stations, samples = waveforms.shape
    rounds = matching.shape[0]
    local = stations // n
    rows = eb * local
    pairs = rounds * eb * eb
    bins, tables = half_tables(samples)
    group = 8 if n % 8 == 0 else 2
    wide = samples + stations
    bf, f32 = jnp.bfloat16, jnp.float32
    vmem, dma = pltpu.VMEM, pltpu.SemaphoreType.DMA
    anywhere = pl.BlockSpec(memory_space=pl.ANY)
    stacks, scores = pl.pallas_call(
        functools.partial(
            kernel, n, eb, rounds, local, stations, samples, bins, group,
            2.0 / math.sqrt(samples * stations),
        ),
        out_shape=(
            jax.ShapeDtypeStruct((n, rows, samples), bf),
            jax.ShapeDtypeStruct((rounds, eb, eb, LAGS), f32),
        ),
        in_specs=[
            pl.BlockSpec(memory_space=pltpu.SMEM),
            pl.BlockSpec(memory_space=pltpu.VMEM),
        ] + [anywhere] * 5,
        out_specs=(anywhere, pl.BlockSpec(memory_space=pltpu.VMEM)),
        scratch_shapes=[
            vmem((eb, stations, samples), bf),
            vmem((n, rows, wide), bf),
            vmem((n, rows, wide), bf),
            vmem(tables[0].shape, bf),
            vmem(tables[1].shape, bf),
            vmem(tables[2].shape, bf),
            vmem(tables[3].shape, bf),
            vmem((n * eb, local, 2 * bins), f32),
            vmem((n * rounds * eb, rows, 2 * bins), bf),
            vmem((n, pairs, LAGS), f32),
            vmem((n, pairs, LAGS), f32),
            vmem((n, pairs, LAGS), f32),
            vmem((n, pairs, 2 * bins), f32),
            vmem((n, rows, 2 * bins), bf),
            vmem((n, rows, samples), bf),
            dma((4,)),
            dma((2,)),
        ] + [dma((n,))] * 8,
        compiler_params=pltpu.CompilerParams(
            collective_id=0, has_side_effects=True, vmem_limit_bytes=56 * 1024 * 1024
        ),
    )(matching, available.transpose(0, 2, 3, 1), waveforms, *(jnp.asarray(t) for t in tables))
    steps = 2 if n % 4 == 0 else 1
    whole = pl.BlockSpec(scores.shape, lambda i: (0, 0, 0, 0))
    return pl.pallas_call(
        functools.partial(finish, eb, local),
        grid=(steps,),
        out_shape=(
            jax.ShapeDtypeStruct((eb, stations, samples), bf),
            jax.ShapeDtypeStruct(scores.shape, f32),
        ),
        in_specs=[pl.BlockSpec((n // steps, rows, samples), lambda i: (i, 0, 0)), whole],
        out_specs=(
            pl.BlockSpec((eb, stations // steps, samples), lambda i: (0, i, 0)), whole
        ),
    )(stacks, scores)


def plain_body(waveforms, matching, available):
    eb, stations, samples = waveforms.shape
    mlen = transform_length(samples)
    forward, corr_tab, spread_tab, back_tab = (jnp.asarray(t) for t in full_tables(samples))
    rounds = matching.shape[0]
    flags = available.astype(jnp.bfloat16)
    held = lax.all_to_all(waveforms, "events", split_axis=1, concat_axis=0, tiled=True)
    held_flags = lax.all_to_all(flags, "events", split_axis=1, concat_axis=0, tiled=True)
    count, local = held.shape[:2]
    blocks = count // eb
    spectra = jnp.dot(
        held.reshape(count * local, samples), forward, preferred_element_type=jnp.float32
    )
    spectra = spectra.astype(jnp.bfloat16).reshape(count, local, 2 * mlen)
    chosen = (matching[:, :, None] == jnp.arange(blocks)[None, None, :]).astype(jnp.bfloat16)
    other = jnp.dot(
        chosen.reshape(rounds * blocks, blocks), spectra.reshape(blocks, eb * local * 2 * mlen),
        preferred_element_type=jnp.float32,
    ).reshape(rounds, blocks, 1, eb, local, 2 * mlen)
    own = spectra.reshape(1, blocks, eb, 1, local, 2 * mlen).astype(jnp.float32)
    real_a, imag_a = (own[..., :mlen], own[..., mlen:])
    real_b, imag_b = (other[..., :mlen], other[..., mlen:])
    cross = jnp.concatenate(
        [real_a * real_b + imag_a * imag_b, real_a * imag_b - imag_a * real_b], axis=-1
    ).astype(jnp.bfloat16)
    corr = jnp.dot(cross.reshape(-1, 2 * mlen), corr_tab, preferred_element_type=jnp.float32)
    corr = corr.reshape(rounds, count, eb, local, LAGS)
    weight_flags = jnp.transpose(held_flags, (2, 0, 3, 1)).astype(jnp.float32)
    totals = lax.psum(jnp.sum(weight_flags[..., None] * corr, axis=3), "events")
    all_scores = totals * (2.0 / math.sqrt(samples * stations))
    all_weights = jax.nn.softmax(all_scores, axis=-1).astype(jnp.bfloat16)
    scores = lax.dynamic_slice_in_dim(all_scores, lax.axis_index("events") * eb, eb, 1)
    spread = jnp.dot(all_weights.reshape(-1, LAGS), spread_tab, preferred_element_type=jnp.float32)
    spread = spread.reshape(rounds, blocks, eb, eb, 1, 2 * mlen)
    real_v, imag_v = (spread[..., :mlen], spread[..., mlen:])
    real_z = jnp.sum(real_v * real_b - imag_v * imag_b, axis=(0, 3))
    imag_z = jnp.sum(real_v * imag_b + imag_v * real_b, axis=(0, 3))
    zspec = jnp.concatenate([real_z, imag_z], axis=-1).astype(jnp.bfloat16)
    stacked = jnp.dot(zspec.reshape(-1, 2 * mlen), back_tab, preferred_element_type=jnp.float32)
    stacked = stacked.reshape(count, local, samples).astype(jnp.bfloat16)
    returned = lax.all_to_all(stacked, "events", split_axis=0, concat_axis=1, tiled=True)
    return (returned, scores)


def solution(mesh):
    n = mesh.shape["events"]
    placed = (
        P(("groups", "events"), None, None),
        P(None, "groups"),
        P(("groups", "events"), None, None, None),
    )

    def body(waveforms, matching, available):
        eb, stations, _ = waveforms.shape
        local = stations // n
        pairs = matching.shape[0] * eb * eb
        if n % 2 == 0 and stations % n == 0 and local % 8 == 0 and 8 <= pairs <= eb * local and (
            eb * local % 16 == 0 and stations % LANES == 0
        ):
            return kernel_body(n, waveforms, matching, available)
        return plain_body(waveforms, matching, available)

    return jax.shard_map(
        body,
        mesh=mesh,
        in_specs=placed,
        out_specs=(P(("groups", "events"), None, None), P(None, ("groups", "events"), None, None)),
        check_vma=False,
    )
```
